32 devices in a mesh: groups: 2 (over y), span: 4 (over z), batch: 4 (over x, core).
Axes of the slice: x: 2, y: 2, z: 4, core: 2. Of those that a mesh axis runs over, the one named last changes fastest.
Arguments:
- embeddings: bfloat16 [8, 512, 768], P(('groups', 'batch'), 'span'), parts along dimension 0, may hold values from -3500 to 3500
- cluster_ids: int32 [8, 512], P(('groups', 'batch'), 'span'), parts along dimension 0, may hold values from 0 to 15, as said below
Outputs:
- nearest: float32 [8, 512], P(('groups', 'batch'), 'span'), parts along dimension 0
The draws below stay inside these ranges and needn't reach their ends.
There are 2 independent parts, one for each index of `groups`. The reference program is written for one: setup_inputs(seed, part) draws one part's arguments, and reference() takes and returns one part's arrays. A program takes and returns all parts, laid end to end along the dimension named above; each array names one. Nothing has to cross between parts.
Inputs may be any that keep to these rules, and one draw needn't show every extreme that they name: `cluster_ids`: on one device at most 96 rows carry ids of one residue modulo 4; in every batch some residue has exactly 96 rows on every device of the span.
All inputs are finite; a program needn't handle non-finite values.
Results may differ from the reference program's by a relative error of at most 0.00061.
Values may be sent and summed in bfloat16 or wider, within the bound.
A program may use at most 64 MiB of HBM per device.

```python
import math
import jax
import jax.numpy as jnp
from jax import lax

D = 768
ROWS_DEV = 128
CLUS_DEV = 4
SPAN_DEVS = 4
BATCHES = 4
SPAN_ROWS = 512
CLUSTERS = 16
CAP = 96


def cluster_layout(key):
    heavy_owner = jax.random.randint(jax.random.fold_in(key, 11), (BATCHES,), 0, SPAN_DEVS)
    offsets = jax.random.randint(jax.random.fold_in(key, 12), (BATCHES, SPAN_DEVS), 0, SPAN_DEVS - 1)
    position = jnp.arange(ROWS_DEV, dtype=jnp.int32)
    others = (heavy_owner[:, None, None] + 1 + (position[None, None, :] - CAP + offsets[:, :, None]) % (SPAN_DEVS - 1)) % SPAN_DEVS
    owners = jnp.where(position[None, None, :] < CAP, heavy_owner[:, None, None], others)
    layers = jax.random.randint(jax.random.fold_in(key, 13), (BATCHES, SPAN_DEVS, ROWS_DEV), 0, CLUS_DEV)
    local_ids = owners + SPAN_DEVS * layers
    ranking = jax.random.randint(jax.random.fold_in(key, 14), (BATCHES, SPAN_DEVS, ROWS_DEV), 0, 1 << 20)
    shuffle = jnp.argsort(ranking * ROWS_DEV + position[None, None, :], axis=-1, stable=True)
    mixed = jnp.take_along_axis(local_ids, shuffle, axis=-1)
    return mixed.reshape(BATCHES, SPAN_ROWS).astype(jnp.int32)


def pick_rows(table, members):
    return table[members]


def draw_cluster_ids(key, part):
    return cluster_layout(key)


def draw_embeddings(key, part):
    members = cluster_layout(key)
    centres = jnp.clip(jax.random.normal(jax.random.fold_in(key, 21), (BATCHES, CLUSTERS, D), jnp.float32), -5.0, 5.0)
    picked = jax.vmap(pick_rows)(centres, members)
    jitter = jnp.clip(jax.random.normal(jax.random.fold_in(key, 22), (BATCHES, SPAN_ROWS, D), jnp.float32), -5.0, 5.0)
    spread = jnp.exp(jax.random.uniform(jax.random.fold_in(key, 23), (BATCHES, SPAN_ROWS, 1), jnp.float32, math.log(0.2), math.log(2.0)))
    columns = jnp.exp(jax.random.uniform(jax.random.fold_in(key, 24), (D,), jnp.float32, 0.0, math.log(10.0)))
    amplitude = jnp.exp(jax.random.uniform(jax.random.fold_in(key, 26), (BATCHES, SPAN_ROWS, 1), jnp.float32, 0.0, math.log(10.0)))
    return (amplitude * (picked + spread * jitter) * columns).astype(jnp.bfloat16)


def setup_inputs(seed: int = 0, part: int = 0) -> dict:
    seeds = jax.random.split(jax.random.key(seed), 3)
    part_keys = jax.random.split(jax.random.fold_in(seeds[2], part), 3)
    embeddings = draw_embeddings(jax.random.fold_in(jax.random.fold_in(seeds[2], part), 71), part)
    cluster_ids = draw_cluster_ids(jax.random.fold_in(jax.random.fold_in(seeds[2], part), 71), part)
    return {"embeddings": embeddings, "cluster_ids": cluster_ids}


def normalize(embeddings):
    values = embeddings.astype(jnp.float32)
    inverse = lax.rsqrt(lax.optimization_barrier(jnp.mean(values * values, axis=-1, keepdims=True)) + 1e-06)
    return (values * inverse * (1.0 / math.sqrt(values.shape[-1]))).astype(jnp.bfloat16)

def batch_nearest(normed, members):
    total_rows = normed.shape[0]
    block_count = total_rows // ROWS_DEV
    column_index = jnp.arange(total_rows, dtype=jnp.int32)

    def one_block(block_number):
        first_row = (block_number * ROWS_DEV).astype(jnp.int32)
        rows_block = lax.dynamic_slice_in_dim(normed, first_row, ROWS_DEV, 0)
        ids_block = lax.dynamic_slice_in_dim(members, first_row, ROWS_DEV, 0)
        scores = lax.dot_general(rows_block, normed, (((1,), (1,)), ((), ())), preferred_element_type=jnp.float32)
        row_index = first_row + jnp.arange(ROWS_DEV, dtype=jnp.int32)
        same_cluster = (ids_block[:, None] == members[None, :]) & (row_index[:, None] != column_index[None, :])
        return lax.optimization_barrier(jnp.max(jnp.where(same_cluster, scores, -1.0), axis=1))
    return lax.map(one_block, jnp.arange(block_count, dtype=jnp.int32)).reshape(total_rows)

def per_batch(inputs):
    return batch_nearest(inputs[0], inputs[1])

def reference(embeddings, cluster_ids):
    normed = normalize(embeddings)
    return lax.map(per_batch, (normed, cluster_ids))
```

```python
import functools
import math

import jax
import jax.numpy as jnp
from jax import lax
from jax.experimental import pallas as pl
from jax.experimental.pallas import tpu as pltpu
from jax.sharding import PartitionSpec as P

MESH = pl.DeviceIdType.MESH
HUB_SPAN = 8


def normalize(embeddings):
    values = embeddings.astype(jnp.float32)
    inverse = lax.rsqrt(jnp.mean(values * values, axis=-1, keepdims=True) + 1e-06)
    return (values * inverse * (1.0 / math.sqrt(values.shape[-1]))).astype(jnp.bfloat16)


def pair_scores(left, right):
    return lax.dot_general(
        left, right, (((1,), (1,)), ((), ())), preferred_element_type=jnp.float32
    )


def gather_device(embeddings, cluster_ids):
    normed = normalize(embeddings[0])
    member_ids = cluster_ids[0]
    row_count = normed.shape[0]
    own_index = lax.axis_index("span")
    own_rows = own_index * row_count + jnp.arange(row_count, dtype=jnp.int32)
    piece_rows = lax.all_gather(normed, "span", axis=0, tiled=True)
    piece_ids = lax.all_gather(member_ids.astype(jnp.bfloat16), "span", axis=0, tiled=True)
    scores = pair_scores(normed, piece_rows)
    column_rows = jnp.arange(piece_rows.shape[0], dtype=jnp.int32)
    same_cluster = (member_ids[:, None] == piece_ids.astype(jnp.int32)[None, :]) & (
        own_rows[:, None] != column_rows[None, :]
    )
    nearest = jnp.max(jnp.where(same_cluster, scores, -1.0), axis=1)
    return jnp.maximum(nearest, -1.0)[None, :]


def hub_kernel(span, emb_ref, ids_ref, out_ref, raw, ids, normed, maxima,
               local_sem, send_sem, ids_send, row_sem, id_sem, back_send, back_sem):
    rows = emb_ref.shape[1]
    me = lax.axis_index("span")
    flip = lax.rem(lax.axis_index("batch"), 2)
    place = jnp.where(flip == 0, me, span - 1 - me)
    hub = span // 2

    def device(spot):
        return {"span": jnp.where(flip == 0, spot, span - 1 - spot)}

    def row_copy(spot):
        return pltpu.make_async_remote_copy(
            src_ref=emb_ref.at[0], dst_ref=raw.at[spot], send_sem=send_sem,
            recv_sem=row_sem.at[spot], device_id=device(hub), device_id_type=MESH)

    def id_copy(spot):
        return pltpu.make_async_remote_copy(
            src_ref=ids_ref, dst_ref=ids.at[spot], send_sem=ids_send,
            recv_sem=id_sem.at[spot], device_id=device(hub), device_id_type=MESH)

    def back_copy(spot):
        return pltpu.make_async_remote_copy(
            src_ref=maxima.at[spot], dst_ref=out_ref, send_sem=back_send.at[spot],
            recv_sem=back_sem, device_id=device(spot), device_id_type=MESH)

    barrier = pltpu.get_barrier_semaphore()

    @pl.when(place != hub)
    def _():
        pl.semaphore_signal(barrier, inc=1, device_id=device(hub), device_id_type=MESH)
        pl.semaphore_wait(barrier, 1)
        id_copy(place).start()
        row_copy(place).start()
        id_copy(place).wait_send()
        row_copy(place).wait_send()
        back_copy(place).wait_recv()

    @pl.when(place == hub)
    def _():
        others = [spot for spot in range(span) if spot != hub]
        for spot in others:
            pl.semaphore_signal(barrier, inc=1, device_id=device(spot), device_id_type=MESH)
        own = pltpu.make_async_copy(emb_ref.at[0], raw.at[hub], local_sem.at[0])
        own_ids = pltpu.make_async_copy(ids_ref, ids.at[hub], local_sem.at[1])
        own.start()
        own_ids.start()
        order = sorted(range(span), key=lambda spot: (abs(spot - hub), -spot))
        row_ids, column_ids, best = [], [], []
        for step, spot in enumerate(order):
            if step == 0:
                own.wait()
                own_ids.wait()
            else:
                if step == 1:
                    pl.semaphore_wait(barrier, span - 1)
                id_copy(spot).wait_recv()
                row_copy(spot).wait_recv()
            row_ids.append(ids[spot])
            column_ids.append(jnp.transpose(jnp.broadcast_to(ids[spot], (rows, rows))))
            block = normalize(raw[spot])
            normed[pl.ds(step * rows, rows), :] = block
            into = pair_scores(normed[pl.ds(0, (step + 1) * rows), :], block)
            apart = lax.broadcasted_iota(jnp.int32, (rows, rows), 0) != \
                lax.broadcasted_iota(jnp.int32, (rows, rows), 1)
            mine = jnp.where((column_ids[step] == row_ids[step]) & apart,
                             into[step * rows:, :], -1.0)
            for other in range(step):
                part = into[other * rows:(other + 1) * rows, :]
                mine = jnp.maximum(
                    mine, jnp.where(column_ids[other] == row_ids[step], part, -1.0))
            best.append(jnp.max(mine, axis=0, keepdims=True))
            if step:
                onto = pair_scores(block, normed[pl.ds(0, step * rows), :])
                for other in range(step):
                    part = onto[:, other * rows:(other + 1) * rows]
                    part = jnp.where(column_ids[step] == row_ids[other], part, -1.0)
                    best[other] = jnp.maximum(
                        best[other], jnp.max(part, axis=0, keepdims=True))
        for step, spot in reversed(list(enumerate(order))):
            if step:
                maxima[spot] = best[step]
                back_copy(spot).start()
        out_ref[...] = best[0]
        for spot in others:
            back_copy(spot).wait_send()


def hub_device(span, embeddings, cluster_ids):
    _, rows, width = embeddings.shape
    return pl.pallas_call(
        functools.partial(hub_kernel, span),
        out_shape=jax.ShapeDtypeStruct((1, rows), jnp.float32),
        in_specs=[pl.BlockSpec(memory_space=pl.ANY)] * 2,
        out_specs=pl.BlockSpec(memory_space=pltpu.VMEM),
        scratch_shapes=[
            pltpu.VMEM((span, rows, width), jnp.bfloat16),
            pltpu.VMEM((span, 1, rows), jnp.int32),
            pltpu.VMEM((span * rows, width), jnp.bfloat16),
            pltpu.VMEM((span, 1, rows), jnp.float32),
            pltpu.SemaphoreType.DMA((2,)),
            pltpu.SemaphoreType.DMA,
            pltpu.SemaphoreType.DMA,
            pltpu.SemaphoreType.DMA((span,)),
            pltpu.SemaphoreType.DMA((span,)),
            pltpu.SemaphoreType.DMA((span,)),
            pltpu.SemaphoreType.DMA,
        ],
        compiler_params=pltpu.CompilerParams(
            collective_id=0, has_side_effects=True, vmem_limit_bytes=16 * 1024 * 1024),
    )(embeddings, cluster_ids)


def solution(mesh):
    span = mesh.shape["span"]
    body = functools.partial(hub_device, span) if 1 < span <= HUB_SPAN else gather_device
    return jax.shard_map(
        body,
        mesh=mesh,
        in_specs=(P(("groups", "batch"), "span", None), P(("groups", "batch"), "span")),
        out_specs=P(("groups", "batch"), "span"),
        check_vma=False,
    )
```

```python
import functools
import math

import jax
import jax.numpy as jnp
from jax import lax
from jax.experimental import pallas as pl
from jax.experimental.pallas import tpu as pltpu
from jax.sharding import PartitionSpec as P

MESH = pl.DeviceIdType.MESH
HUB_SPAN = 8


def normalize(embeddings):
    values = embeddings.astype(jnp.float32)
    inverse = lax.rsqrt(jnp.mean(values * values, axis=-1, keepdims=True) + 1e-06)
    return (values * inverse * (1.0 / math.sqrt(values.shape[-1]))).astype(jnp.bfloat16)


def pair_scores(left, right):
    return lax.dot_general(
        left, right, (((1,), (1,)), ((), ())), preferred_element_type=jnp.float32
    )


def gather_device(embeddings, cluster_ids):
    normed = normalize(embeddings[0])
    member_ids = cluster_ids[0]
    row_count = normed.shape[0]
    own_index = lax.axis_index("span")
    own_rows = own_index * row_count + jnp.arange(row_count, dtype=jnp.int32)
    piece_rows = lax.all_gather(normed, "span", axis=0, tiled=True)
    piece_ids = lax.all_gather(member_ids.astype(jnp.bfloat16), "span", axis=0, tiled=True)
    scores = pair_scores(normed, piece_rows)
    column_rows = jnp.arange(piece_rows.shape[0], dtype=jnp.int32)
    same_cluster = (member_ids[:, None] == piece_ids.astype(jnp.int32)[None, :]) & (
        own_rows[:, None] != column_rows[None, :]
    )
    nearest = jnp.max(jnp.where(same_cluster, scores, -1.0), axis=1)
    return jnp.maximum(nearest, -1.0)[None, :]


def hub_kernel(span, emb_ref, ids_ref, out_ref, raw, ids, normed, maxima,
               local_sem, send_sem, ids_send, row_sem, id_sem, back_send, back_sem):
    rows = emb_ref.shape[1]
    me = lax.axis_index("span")
    flip = 1 - lax.rem(lax.axis_index("batch"), 2)
    place = jnp.where(flip == 0, me, span - 1 - me)
    hub = span // 2

    def device(spot):
        return {"span": jnp.where(flip == 0, spot, span - 1 - spot)}

    def row_copy(spot):
        return pltpu.make_async_remote_copy(
            src_ref=emb_ref.at[0], dst_ref=raw.at[spot], send_sem=send_sem,
            recv_sem=row_sem.at[spot], device_id=device(hub), device_id_type=MESH)

    def id_copy(spot):
        return pltpu.make_async_remote_copy(
            src_ref=ids_ref, dst_ref=ids.at[spot], send_sem=ids_send,
            recv_sem=id_sem.at[spot], device_id=device(hub), device_id_type=MESH)

    def back_copy(spot):
        return pltpu.make_async_remote_copy(
            src_ref=maxima.at[spot], dst_ref=out_ref, send_sem=back_send.at[spot],
            recv_sem=back_sem, device_id=device(spot), device_id_type=MESH)

    barrier = pltpu.get_barrier_semaphore()

    @pl.when(place != hub)
    def _():
        pl.semaphore_signal(barrier, inc=1, device_id=device(hub), device_id_type=MESH)
        pl.semaphore_wait(barrier, 1)
        id_copy(place).start()
        row_copy(place).start()
        id_copy(place).wait_send()
        row_copy(place).wait_send()
        back_copy(place).wait_recv()

    @pl.when(place == hub)
    def _():
        others = [spot for spot in range(span) if spot != hub]
        for spot in others:
            pl.semaphore_signal(barrier, inc=1, device_id=device(spot), device_id_type=MESH)
        own = pltpu.make_async_copy(emb_ref.at[0], raw.at[hub], local_sem.at[0])
        own_ids = pltpu.make_async_copy(ids_ref, ids.at[hub], local_sem.at[1])
        own.start()
        own_ids.start()
        order = sorted(range(span), key=lambda spot: (abs(spot - hub), -spot))
        row_ids, column_ids, best = [], [], []
        for step, spot in enumerate(order):
            if step == 0:
                own.wait()
                own_ids.wait()
            else:
                if step == 1:
                    pl.semaphore_wait(barrier, span - 1)
                id_copy(spot).wait_recv()
                row_copy(spot).wait_recv()
            row_ids.append(ids[spot])
            column_ids.append(jnp.transpose(jnp.broadcast_to(ids[spot], (rows, rows))))
            block = normalize(raw[spot])
            normed[pl.ds(step * rows, rows), :] = block
            into = pair_scores(normed[pl.ds(0, (step + 1) * rows), :], block)
            apart = lax.broadcasted_iota(jnp.int32, (rows, rows), 0) != \
                lax.broadcasted_iota(jnp.int32, (rows, rows), 1)
            mine = jnp.where((column_ids[step] == row_ids[step]) & apart,
                             into[step * rows:, :], -1.0)
            for other in range(step):
                part = into[other * rows:(other + 1) * rows, :]
                mine = jnp.maximum(
                    mine, jnp.where(column_ids[other] == row_ids[step], part, -1.0))
            best.append(jnp.max(mine, axis=0, keepdims=True))
            if step:
                onto = pair_scores(block, normed[pl.ds(0, step * rows), :])
                for other in range(step):
                    part = onto[:, other * rows:(other + 1) * rows]
                    part = jnp.where(column_ids[step] == row_ids[other], part, -1.0)
                    best[other] = jnp.maximum(
                        best[other], jnp.max(part, axis=0, keepdims=True))
        for step, spot in reversed(list(enumerate(order))):
            if step:
                maxima[spot] = best[step]
                back_copy(spot).start()
        out_ref[...] = best[0]
        for spot in others:
            back_copy(spot).wait_send()


def hub_device(span, embeddings, cluster_ids):
    _, rows, width = embeddings.shape
    return pl.pallas_call(
        functools.partial(hub_kernel, span),
        out_shape=jax.ShapeDtypeStruct((1, rows), jnp.float32),
        in_specs=[pl.BlockSpec(memory_space=pl.ANY)] * 2,
        out_specs=pl.BlockSpec(memory_space=pltpu.VMEM),
        scratch_shapes=[
            pltpu.VMEM((span, rows, width), jnp.bfloat16),
            pltpu.VMEM((span, 1, rows), jnp.int32),
            pltpu.VMEM((span * rows, width), jnp.bfloat16),
            pltpu.VMEM((span, 1, rows), jnp.float32),
            pltpu.SemaphoreType.DMA((2,)),
            pltpu.SemaphoreType.DMA,
            pltpu.SemaphoreType.DMA,
            pltpu.SemaphoreType.DMA((span,)),
            pltpu.SemaphoreType.DMA((span,)),
            pltpu.SemaphoreType.DMA((span,)),
            pltpu.SemaphoreType.DMA,
        ],
        compiler_params=pltpu.CompilerParams(
            collective_id=0, has_side_effects=True, vmem_limit_bytes=60 * 1024 * 1024),
    )(embeddings, cluster_ids)


def solution(mesh):
    span = mesh.shape["span"]
    body = functools.partial(hub_device, span) if 1 < span <= HUB_SPAN else gather_device
    return jax.shard_map(
        body,
        mesh=mesh,
        in_specs=(P(("groups", "batch"), "span", None), P(("groups", "batch"), "span")),
        out_specs=P(("groups", "batch"), "span"),
        check_vma=False,
    )
```

```python
import functools
import math

import jax
import jax.numpy as jnp
from jax import lax
from jax.experimental import pallas as pl
from jax.experimental.pallas import tpu as pltpu
from jax.sharding import PartitionSpec as P

MESH = pl.DeviceIdType.MESH
HUB_SPAN = 8
PIECES = 2


def normalize(embeddings):
    values = embeddings.astype(jnp.float32)
    inverse = lax.rsqrt(jnp.mean(values * values, axis=-1, keepdims=True) + 1e-06)
    return (values * inverse * (1.0 / math.sqrt(values.shape[-1]))).astype(jnp.bfloat16)


def pair_scores(left, right):
    return lax.dot_general(
        left, right, (((1,), (1,)), ((), ())), preferred_element_type=jnp.float32
    )


def gather_device(embeddings, cluster_ids):
    normed = normalize(embeddings[0])
    member_ids = cluster_ids[0]
    row_count = normed.shape[0]
    own_index = lax.axis_index("span")
    own_rows = own_index * row_count + jnp.arange(row_count, dtype=jnp.int32)
    piece_rows = lax.all_gather(normed, "span", axis=0, tiled=True)
    piece_ids = lax.all_gather(member_ids.astype(jnp.bfloat16), "span", axis=0, tiled=True)
    scores = pair_scores(normed, piece_rows)
    column_rows = jnp.arange(piece_rows.shape[0], dtype=jnp.int32)
    same_cluster = (member_ids[:, None] == piece_ids.astype(jnp.int32)[None, :]) & (
        own_rows[:, None] != column_rows[None, :]
    )
    nearest = jnp.max(jnp.where(same_cluster, scores, -1.0), axis=1)
    return jnp.maximum(nearest, -1.0)[None, :]


def masked_pairs(scores, column_ids, row_ids):
    return jnp.where(column_ids == row_ids, scores, -1.0)


def as_columns(row):
    return jnp.transpose(jnp.broadcast_to(row, (row.shape[1], row.shape[1])))


def within(block, column_ids, row_ids):
    rows = block.shape[0]
    apart = lax.broadcasted_iota(jnp.int32, (rows, rows), 0) != \
        lax.broadcasted_iota(jnp.int32, (rows, rows), 1)
    pairs = masked_pairs(pair_scores(block, block), column_ids, row_ids)
    return jnp.max(jnp.where(apart, pairs, -1.0), axis=0, keepdims=True)


def hub_kernel(span, pieces, emb_ref, ids_ref, out_ref, raw, ids, normed, maxima, back,
               local_sem, local_ids, send_sem, ids_send, row_sem, id_sem, back_send, back_sem):
    rows = emb_ref.shape[1]
    part = rows // pieces
    me = lax.axis_index("span")
    flip = lax.rem(lax.axis_index("batch"), 2)
    place = jnp.where(flip == 1, me, span - 1 - me)
    hub = span // 2

    def device(spot):
        return {"span": jnp.where(flip == 1, spot, span - 1 - spot)}

    def local_copy(piece):
        cut = pl.ds(piece * part, part)
        return pltpu.make_async_copy(
            emb_ref.at[0, cut], raw.at[place, cut], local_sem.at[piece])

    def local_id_copy():
        return pltpu.make_async_copy(ids_ref, ids.at[place], local_ids)

    def row_copy(spot, piece):
        cut = pl.ds(piece * part, part)
        return pltpu.make_async_remote_copy(
            src_ref=raw.at[spot, cut], dst_ref=raw.at[spot, cut], send_sem=send_sem.at[piece],
            recv_sem=row_sem.at[spot, piece], device_id=device(hub), device_id_type=MESH)

    def id_copy(spot):
        return pltpu.make_async_remote_copy(
            src_ref=ids.at[spot], dst_ref=ids.at[spot], send_sem=ids_send,
            recv_sem=id_sem.at[spot], device_id=device(hub), device_id_type=MESH)

    def back_copy(spot):
        return pltpu.make_async_remote_copy(
            src_ref=maxima.at[spot], dst_ref=back, send_sem=back_send.at[spot],
            recv_sem=back_sem, device_id=device(spot), device_id_type=MESH)

    barrier = pltpu.get_barrier_semaphore()
    local_id_copy().start()
    for piece in range(pieces):
        local_copy(piece).start()

    @pl.when(place != hub)
    def _():
        pl.semaphore_signal(barrier, inc=1, device_id=device(hub), device_id_type=MESH)
        local_id_copy().wait()
        local_copy(0).wait()
        pl.semaphore_wait(barrier, 1)
        id_copy(place).start()
        row_copy(place, 0).start()
        for piece in range(1, pieces):
            local_copy(piece).wait()
            row_copy(place, piece).start()
        own_ids = ids[place]
        own = within(normalize(raw[place]), as_columns(own_ids), own_ids)
        id_copy(place).wait_send()
        for piece in range(pieces):
            row_copy(place, piece).wait_send()
        back_copy(place).wait_recv()
        out_ref[...] = jnp.maximum(back[...], own)

    @pl.when(place == hub)
    def _():
        others = [spot for spot in range(span) if spot != hub]
        for spot in others:
            pl.semaphore_signal(barrier, inc=1, device_id=device(spot), device_id_type=MESH)
        local_id_copy().wait()
        for piece in range(pieces):
            local_copy(piece).wait()
        order = sorted(range(span), key=lambda spot: (abs(spot - hub), -spot))
        row_ids = [ids[hub]]
        block = normalize(raw[hub])
        normed[pl.ds(0, rows), :] = block
        best = [within(block, as_columns(row_ids[0]), row_ids[0])]
        pl.semaphore_wait(barrier, span - 1)
        for spot in order[1:]:
            id_copy(spot).wait_recv()
            row_ids.append(ids[spot])
        column_ids = [as_columns(row) for row in row_ids]
        for step, spot in list(enumerate(order))[1:]:
            across = []
            for piece in range(pieces):
                cut = slice(piece * part, (piece + 1) * part)
                row_copy(spot, piece).wait_recv()
                block = normalize(raw[spot, cut])
                if step < span - 1:
                    normed[pl.ds(step * rows + piece * part, part), :] = block
                scores = pair_scores(block, normed[pl.ds(0, step * rows), :])
                widest = None
                for other in range(step):
                    pairs = masked_pairs(scores[:, other * rows:(other + 1) * rows],
                                         column_ids[step][cut], row_ids[other])
                    best[other] = jnp.maximum(
                        best[other], jnp.max(pairs, axis=0, keepdims=True))
                    widest = pairs if widest is None else jnp.maximum(widest, pairs)
                across.append(widest)
            widest = jnp.transpose(jnp.concatenate(across, axis=0))
            best.append(jnp.max(widest, axis=0, keepdims=True))
        for step, spot in reversed(list(enumerate(order))):
            if step:
                maxima[spot] = best[step]
                back_copy(spot).start()
        out_ref[...] = best[0]
        for spot in others:
            back_copy(spot).wait_send()


def hub_device(span, embeddings, cluster_ids):
    _, rows, width = embeddings.shape
    pieces = PIECES if rows % (16 * PIECES) == 0 else 1
    return pl.pallas_call(
        functools.partial(hub_kernel, span, pieces),
        out_shape=pltpu.VMEM((1, rows), jnp.float32),
        in_specs=[pl.BlockSpec(memory_space=pl.ANY)] * 2,
        out_specs=pl.BlockSpec(memory_space=pltpu.VMEM),
        scratch_shapes=[
            pltpu.VMEM((span, rows, width), jnp.bfloat16),
            pltpu.VMEM((span, 1, rows), jnp.int32),
            pltpu.VMEM(((span - 1) * rows, width), jnp.bfloat16),
            pltpu.VMEM((span, 1, rows), jnp.float32),
            pltpu.VMEM((1, rows), jnp.float32),
            pltpu.SemaphoreType.DMA((pieces,)),
            pltpu.SemaphoreType.DMA,
            pltpu.SemaphoreType.DMA((pieces,)),
            pltpu.SemaphoreType.DMA,
            pltpu.SemaphoreType.DMA((span, pieces)),
            pltpu.SemaphoreType.DMA((span,)),
            pltpu.SemaphoreType.DMA((span,)),
            pltpu.SemaphoreType.DMA,
        ],
        compiler_params=pltpu.CompilerParams(
            collective_id=0, has_side_effects=True, vmem_limit_bytes=60 * 1024 * 1024),
    )(embeddings, cluster_ids)


def solution(mesh):
    span = mesh.shape["span"]
    body = functools.partial(hub_device, span) if 1 < span <= HUB_SPAN else gather_device
    return jax.shard_map(
        body,
        mesh=mesh,
        in_specs=(P(("groups", "batch"), "span", None), P(("groups", "batch"), "span")),
        out_specs=P(("groups", "batch"), "span"),
        check_vma=False,
    )
```

```python
import functools
import math

import jax
import jax.numpy as jnp
from jax import lax
from jax.experimental import pallas as pl
from jax.experimental.pallas import tpu as pltpu
from jax.sharding import PartitionSpec as P

MESH = pl.DeviceIdType.MESH
HUB_SPAN = 8
PIECES = 1


def normalize(embeddings):
    values = embeddings.astype(jnp.float32)
    inverse = lax.rsqrt(jnp.mean(values * values, axis=-1, keepdims=True) + 1e-06)
    return (values * inverse * (1.0 / math.sqrt(values.shape[-1]))).astype(jnp.bfloat16)


def pair_scores(left, right):
    return lax.dot_general(
        left, right, (((1,), (1,)), ((), ())), preferred_element_type=jnp.float32
    )


def gather_device(embeddings, cluster_ids):
    normed = normalize(embeddings[0])
    member_ids = cluster_ids[0]
    row_count = normed.shape[0]
    own_index = lax.axis_index("span")
    own_rows = own_index * row_count + jnp.arange(row_count, dtype=jnp.int32)
    piece_rows = lax.all_gather(normed, "span", axis=0, tiled=True)
    piece_ids = lax.all_gather(member_ids.astype(jnp.bfloat16), "span", axis=0, tiled=True)
    scores = pair_scores(normed, piece_rows)
    column_rows = jnp.arange(piece_rows.shape[0], dtype=jnp.int32)
    same_cluster = (member_ids[:, None] == piece_ids.astype(jnp.int32)[None, :]) & (
        own_rows[:, None] != column_rows[None, :]
    )
    nearest = jnp.max(jnp.where(same_cluster, scores, -1.0), axis=1)
    return jnp.maximum(nearest, -1.0)[None, :]


def masked_pairs(scores, column_ids, row_ids):
    return jnp.where(column_ids == row_ids, scores, -1.0)


def as_columns(row):
    return jnp.transpose(jnp.broadcast_to(row, (row.shape[1], row.shape[1])))


def within(block, column_ids, row_ids):
    rows = block.shape[0]
    apart = lax.broadcasted_iota(jnp.int32, (rows, rows), 0) != \
        lax.broadcasted_iota(jnp.int32, (rows, rows), 1)
    pairs = masked_pairs(pair_scores(block, block), column_ids, row_ids)
    return jnp.max(jnp.where(apart, pairs, -1.0), axis=0, keepdims=True)


def hub_kernel(span, pieces, emb_ref, ids_ref, out_ref, raw, ids, normed, maxima, back,
               local_sem, local_ids, send_sem, ids_send, row_sem, id_sem, back_send, back_sem):
    rows = emb_ref.shape[1]
    part = rows // pieces
    me = lax.axis_index("span")
    flip = lax.rem(lax.axis_index("batch"), 2)
    place = jnp.where(flip == 1, me, span - 1 - me)
    hub = span // 2

    def device(spot):
        return {"span": jnp.where(flip == 1, spot, span - 1 - spot)}

    def local_copy(piece):
        cut = pl.ds(piece * part, part)
        return pltpu.make_async_copy(
            emb_ref.at[0, cut], raw.at[place, cut], local_sem.at[piece])

    def local_id_copy():
        return pltpu.make_async_copy(ids_ref, ids.at[place], local_ids)

    def row_copy(spot, piece):
        cut = pl.ds(piece * part, part)
        return pltpu.make_async_remote_copy(
            src_ref=raw.at[spot, cut], dst_ref=raw.at[spot, cut], send_sem=send_sem.at[piece],
            recv_sem=row_sem.at[spot, piece], device_id=device(hub), device_id_type=MESH)

    def id_copy(spot):
        return pltpu.make_async_remote_copy(
            src_ref=ids.at[spot], dst_ref=ids.at[spot], send_sem=ids_send,
            recv_sem=id_sem.at[spot], device_id=device(hub), device_id_type=MESH)

    def back_copy(spot):
        return pltpu.make_async_remote_copy(
            src_ref=maxima.at[spot], dst_ref=back, send_sem=back_send.at[spot],
            recv_sem=back_sem, device_id=device(spot), device_id_type=MESH)

    barrier = pltpu.get_barrier_semaphore()
    local_id_copy().start()
    for piece in range(pieces):
        local_copy(piece).start()

    @pl.when(place != hub)
    def _():
        pl.semaphore_signal(barrier, inc=1, device_id=device(hub), device_id_type=MESH)
        local_id_copy().wait()
        local_copy(0).wait()
        pl.semaphore_wait(barrier, 1)
        id_copy(place).start()
        row_copy(place, 0).start()
        for piece in range(1, pieces):
            local_copy(piece).wait()
            row_copy(place, piece).start()
        own_ids = ids[place]
        own = within(normalize(raw[place]), as_columns(own_ids), own_ids)
        id_copy(place).wait_send()
        for piece in range(pieces):
            row_copy(place, piece).wait_send()
        back_copy(place).wait_recv()
        out_ref[...] = jnp.maximum(back[...], own)

    @pl.when(place == hub)
    def _():
        others = [spot for spot in range(span) if spot != hub]
        for spot in others:
            pl.semaphore_signal(barrier, inc=1, device_id=device(spot), device_id_type=MESH)
        local_id_copy().wait()
        for piece in range(pieces):
            local_copy(piece).wait()
        order = sorted(range(span), key=lambda spot: (abs(spot - hub), -spot))
        row_ids = [ids[hub]]
        block = normalize(raw[hub])
        normed[pl.ds(0, rows), :] = block
        best = [within(block, as_columns(row_ids[0]), row_ids[0])]
        pl.semaphore_wait(barrier, span - 1)
        for spot in order[1:]:
            id_copy(spot).wait_recv()
            row_ids.append(ids[spot])
        column_ids = [as_columns(row) for row in row_ids]
        for step, spot in list(enumerate(order))[1:]:
            across = []
            for piece in range(pieces):
                cut = slice(piece * part, (piece + 1) * part)
                row_copy(spot, piece).wait_recv()
                block = normalize(raw[spot, cut])
                if step < span - 1:
                    normed[pl.ds(step * rows + piece * part, part), :] = block
                scores = pair_scores(block, normed[pl.ds(0, step * rows), :])
                widest = None
                for other in range(step):
                    pairs = masked_pairs(scores[:, other * rows:(other + 1) * rows],
                                         column_ids[step][cut], row_ids[other])
                    best[other] = jnp.maximum(
                        best[other], jnp.max(pairs, axis=0, keepdims=True))
                    widest = pairs if widest is None else jnp.maximum(widest, pairs)
                across.append(widest)
            widest = jnp.transpose(jnp.concatenate(across, axis=0))
            best.append(jnp.max(widest, axis=0, keepdims=True))
        for step, spot in reversed(list(enumerate(order))):
            if step:
                maxima[spot] = best[step]
                back_copy(spot).start()
        out_ref[...] = best[0]
        for spot in others:
            back_copy(spot).wait_send()


def hub_device(span, embeddings, cluster_ids):
    _, rows, width = embeddings.shape
    pieces = PIECES if rows % (16 * PIECES) == 0 else 1
    return pl.pallas_call(
        functools.partial(hub_kernel, span, pieces),
        out_shape=pltpu.VMEM((1, rows), jnp.float32),
        in_specs=[pl.BlockSpec(memory_space=pl.ANY)] * 2,
        out_specs=pl.BlockSpec(memory_space=pltpu.VMEM),
        scratch_shapes=[
            pltpu.VMEM((span, rows, width), jnp.bfloat16),
            pltpu.VMEM((span, 1, rows), jnp.int32),
            pltpu.VMEM(((span - 1) * rows, width), jnp.bfloat16),
            pltpu.VMEM((span, 1, rows), jnp.float32),
            pltpu.VMEM((1, rows), jnp.float32),
            pltpu.SemaphoreType.DMA((pieces,)),
            pltpu.SemaphoreType.DMA,
            pltpu.SemaphoreType.DMA((pieces,)),
            pltpu.SemaphoreType.DMA,
            pltpu.SemaphoreType.DMA((span, pieces)),
            pltpu.SemaphoreType.DMA((span,)),
            pltpu.SemaphoreType.DMA((span,)),
            pltpu.SemaphoreType.DMA,
        ],
        compiler_params=pltpu.CompilerParams(
            collective_id=0, has_side_effects=True, vmem_limit_bytes=60 * 1024 * 1024),
    )(embeddings, cluster_ids)


def solution(mesh):
    span = mesh.shape["span"]
    body = functools.partial(hub_device, span) if 1 < span <= HUB_SPAN else gather_device
    return jax.shard_map(
        body,
        mesh=mesh,
        in_specs=(P(("groups", "batch"), "span", None), P(("groups", "batch"), "span")),
        out_specs=P(("groups", "batch"), "span"),
        check_vma=False,
    )
```

```python
import functools
import math

import jax
import jax.numpy as jnp
from jax import lax
from jax.experimental import pallas as pl
from jax.experimental.pallas import tpu as pltpu
from jax.sharding import PartitionSpec as P

MESH = pl.DeviceIdType.MESH
HUB_SPAN = 8


def normalize(embeddings):
    values = embeddings.astype(jnp.float32)
    inverse = lax.rsqrt(jnp.mean(values * values, axis=-1, keepdims=True) + 1e-06)
    return (values * inverse * (1.0 / math.sqrt(values.shape[-1]))).astype(jnp.bfloat16)


def pair_scores(left, right):
    return lax.dot_general(
        left, right, (((1,), (1,)), ((), ())), preferred_element_type=jnp.float32
    )


def gather_device(embeddings, cluster_ids):
    normed = normalize(embeddings[0])
    member_ids = cluster_ids[0]
    row_count = normed.shape[0]
    own_index = lax.axis_index("span")
    own_rows = own_index * row_count + jnp.arange(row_count, dtype=jnp.int32)
    piece_rows = lax.all_gather(normed, "span", axis=0, tiled=True)
    piece_ids = lax.all_gather(member_ids.astype(jnp.bfloat16), "span", axis=0, tiled=True)
    scores = pair_scores(normed, piece_rows)
    column_rows = jnp.arange(piece_rows.shape[0], dtype=jnp.int32)
    same_cluster = (member_ids[:, None] == piece_ids.astype(jnp.int32)[None, :]) & (
        own_rows[:, None] != column_rows[None, :]
    )
    nearest = jnp.max(jnp.where(same_cluster, scores, -1.0), axis=1)
    return jnp.maximum(nearest, -1.0)[None, :]


def masked_pairs(scores, column_ids, row_ids):
    return jnp.where(column_ids == row_ids, scores, -1.0)


def as_columns(row):
    return jnp.transpose(jnp.broadcast_to(row, (row.shape[1], row.shape[1])))


def within(block, column_ids, row_ids):
    rows = block.shape[0]
    apart = lax.broadcasted_iota(jnp.int32, (rows, rows), 0) != \
        lax.broadcasted_iota(jnp.int32, (rows, rows), 1)
    pairs = masked_pairs(pair_scores(block, block), column_ids, row_ids)
    return jnp.max(jnp.where(apart, pairs, -1.0), axis=0, keepdims=True)


def hub_kernel(span, emb_ref, ids_ref, out_ref, raw, ids, normed, maxima, back,
               local_sem, local_ids, send_sem, ids_send, row_sem, id_sem, back_send, back_sem):
    rows = emb_ref.shape[1]
    me = lax.axis_index("span")
    flip = lax.rem(lax.axis_index("batch"), 2)
    place = jnp.where(flip == 1, me, span - 1 - me)
    hub = span // 2

    def slot(spot):
        away = spot - hub
        if isinstance(spot, int):
            order = min(2 * away - 1 if away > 0 else -2 * away, span - 1)
            return pl.ds(order * rows, rows)
        order = jnp.minimum(jnp.where(away > 0, 2 * away - 1, -2 * away), span - 1)
        return pl.ds(pl.multiple_of(order * rows, rows), rows)

    def device(spot):
        return {"span": jnp.where(flip == 1, spot, span - 1 - spot)}

    def local_copy():
        return pltpu.make_async_copy(emb_ref.at[0], raw, local_sem)

    def local_id_copy():
        return pltpu.make_async_copy(ids_ref, ids.at[place], local_ids)

    def row_copy(spot):
        return pltpu.make_async_remote_copy(
            src_ref=normed.at[slot(spot)], dst_ref=normed.at[slot(spot)], send_sem=send_sem,
            recv_sem=row_sem.at[spot], device_id=device(hub), device_id_type=MESH)

    def id_copy(spot):
        return pltpu.make_async_remote_copy(
            src_ref=ids.at[spot], dst_ref=ids.at[spot], send_sem=ids_send,
            recv_sem=id_sem.at[spot], device_id=device(hub), device_id_type=MESH)

    def back_copy(spot):
        return pltpu.make_async_remote_copy(
            src_ref=maxima.at[spot], dst_ref=back, send_sem=back_send.at[spot],
            recv_sem=back_sem, device_id=device(spot), device_id_type=MESH)

    barrier = pltpu.get_barrier_semaphore()
    local_id_copy().start()
    local_copy().start()

    @pl.when(place != hub)
    def _():
        pl.semaphore_signal(barrier, inc=1, device_id=device(hub), device_id_type=MESH)
        local_id_copy().wait()
        local_copy().wait()
        block = normalize(raw[...])
        normed[slot(place), :] = block
        pl.semaphore_wait(barrier, 1)
        id_copy(place).start()
        row_copy(place).start()
        own_ids = ids[place]
        own = within(block, as_columns(own_ids), own_ids)
        id_copy(place).wait_send()
        row_copy(place).wait_send()
        back_copy(place).wait_recv()
        out_ref[...] = jnp.maximum(back[...], own)

    @pl.when(place == hub)
    def _():
        others = [spot for spot in range(span) if spot != hub]
        for spot in others:
            pl.semaphore_signal(barrier, inc=1, device_id=device(spot), device_id_type=MESH)
        local_id_copy().wait()
        local_copy().wait()
        order = sorted(range(span), key=lambda spot: (abs(spot - hub), -spot))
        row_ids = [ids[hub]]
        block = normalize(raw[...])
        normed[slot(hub), :] = block
        best = [within(block, as_columns(row_ids[0]), row_ids[0])]
        pl.semaphore_wait(barrier, span - 1)
        for spot in order[1:]:
            id_copy(spot).wait_recv()
            row_ids.append(ids[spot])
        column_ids = [as_columns(row) for row in row_ids]
        for step, spot in list(enumerate(order))[1:]:
            row_copy(spot).wait_recv()
            scores = pair_scores(normed[slot(spot), :], normed[pl.ds(0, step * rows), :])
            widest = None
            for other in range(step):
                pairs = masked_pairs(scores[:, other * rows:(other + 1) * rows],
                                     column_ids[step], row_ids[other])
                best[other] = jnp.maximum(
                    best[other], jnp.max(pairs, axis=0, keepdims=True))
                widest = pairs if widest is None else jnp.maximum(widest, pairs)
            best.append(jnp.max(jnp.transpose(widest), axis=0, keepdims=True))
        for step, spot in reversed(list(enumerate(order))):
            if step:
                maxima[spot] = best[step]
                back_copy(spot).start()
        out_ref[...] = best[0]
        for spot in others:
            back_copy(spot).wait_send()


def hub_device(span, embeddings, cluster_ids):
    _, rows, width = embeddings.shape
    return pl.pallas_call(
        functools.partial(hub_kernel, span),
        out_shape=pltpu.VMEM((1, rows), jnp.float32),
        in_specs=[pl.BlockSpec(memory_space=pl.ANY)] * 2,
        out_specs=pl.BlockSpec(memory_space=pltpu.VMEM),
        scratch_shapes=[
            pltpu.VMEM((rows, width), jnp.bfloat16),
            pltpu.VMEM((span, 1, rows), jnp.int32),
            pltpu.VMEM((span * rows, width), jnp.bfloat16),
            pltpu.VMEM((span, 1, rows), jnp.float32),
            pltpu.VMEM((1, rows), jnp.float32),
            pltpu.SemaphoreType.DMA,
            pltpu.SemaphoreType.DMA,
            pltpu.SemaphoreType.DMA,
            pltpu.SemaphoreType.DMA,
            pltpu.SemaphoreType.DMA((span,)),
            pltpu.SemaphoreType.DMA((span,)),
            pltpu.SemaphoreType.DMA((span,)),
            pltpu.SemaphoreType.DMA,
        ],
        compiler_params=pltpu.CompilerParams(
            collective_id=0, has_side_effects=True, vmem_limit_bytes=60 * 1024 * 1024),
    )(embeddings, cluster_ids)


def solution(mesh):
    span = mesh.shape["span"]
    body = functools.partial(hub_device, span) if 1 < span <= HUB_SPAN else gather_device
    return jax.shard_map(
        body,
        mesh=mesh,
        in_specs=(P(("groups", "batch"), "span", None), P(("groups", "batch"), "span")),
        out_specs=P(("groups", "batch"), "span"),
        check_vma=False,
    )
```

```python
import functools
import math

import jax
import jax.numpy as jnp
from jax import lax
from jax.experimental import pallas as pl
from jax.experimental.pallas import tpu as pltpu
from jax.sharding import PartitionSpec as P

MESH = pl.DeviceIdType.MESH
HUB_SPAN = 8


def normalize(embeddings):
    values = embeddings.astype(jnp.float32)
    inverse = lax.rsqrt(jnp.mean(values * values, axis=-1, keepdims=True) + 1e-06)
    return (values * inverse * (1.0 / math.sqrt(values.shape[-1]))).astype(jnp.bfloat16)


def pair_scores(left, right):
    return lax.dot_general(
        left, right, (((1,), (1,)), ((), ())), preferred_element_type=jnp.float32
    )


def gather_device(embeddings, cluster_ids):
    normed = normalize(embeddings[0])
    member_ids = cluster_ids[0]
    row_count = normed.shape[0]
    own_index = lax.axis_index("span")
    own_rows = own_index * row_count + jnp.arange(row_count, dtype=jnp.int32)
    piece_rows = lax.all_gather(normed, "span", axis=0, tiled=True)
    piece_ids = lax.all_gather(member_ids.astype(jnp.bfloat16), "span", axis=0, tiled=True)
    scores = pair_scores(normed, piece_rows)
    column_rows = jnp.arange(piece_rows.shape[0], dtype=jnp.int32)
    same_cluster = (member_ids[:, None] == piece_ids.astype(jnp.int32)[None, :]) & (
        own_rows[:, None] != column_rows[None, :]
    )
    nearest = jnp.max(jnp.where(same_cluster, scores, -1.0), axis=1)
    return jnp.maximum(nearest, -1.0)[None, :]


def masked_pairs(scores, column_ids, row_ids):
    return jnp.where(column_ids == row_ids, scores, -1.0)


def as_columns(row):
    return jnp.transpose(jnp.broadcast_to(row, (row.shape[1], row.shape[1])))


def within(block, column_ids, row_ids):
    rows = block.shape[0]
    apart = lax.broadcasted_iota(jnp.int32, (rows, rows), 0) != \
        lax.broadcasted_iota(jnp.int32, (rows, rows), 1)
    pairs = masked_pairs(pair_scores(block, block), column_ids, row_ids)
    return jnp.max(jnp.where(apart, pairs, -1.0), axis=0, keepdims=True)


def hub_kernel(span, emb_ref, ids_ref, out_ref, raw, ids, normed, maxima, back,
               local_sem, local_ids, send_sem, ids_send, row_sem, id_sem, back_send, back_sem):
    rows = emb_ref.shape[1]
    me = lax.axis_index("span")
    flip = lax.rem(lax.axis_index("batch"), 2)
    place = jnp.where(flip == 1, me, span - 1 - me)
    hub = span // 2

    def slot(spot):
        away = spot - hub
        if isinstance(spot, int):
            order = min(2 * away - 1 if away > 0 else -2 * away, span - 1)
            return pl.ds(order * rows, rows)
        order = jnp.minimum(jnp.where(away > 0, 2 * away - 1, -2 * away), span - 1)
        return pl.ds(pl.multiple_of(order * rows, rows), rows)

    def device(spot):
        return {"span": jnp.where(flip == 1, spot, span - 1 - spot)}

    def local_copy():
        return pltpu.make_async_copy(emb_ref.at[0], raw, local_sem)

    def local_id_copy():
        return pltpu.make_async_copy(ids_ref, ids.at[place], local_ids)

    def row_copy(spot):
        return pltpu.make_async_remote_copy(
            src_ref=normed.at[slot(spot)], dst_ref=normed.at[slot(spot)], send_sem=send_sem,
            recv_sem=row_sem.at[spot], device_id=device(hub), device_id_type=MESH)

    def id_copy(spot):
        return pltpu.make_async_remote_copy(
            src_ref=ids.at[spot], dst_ref=ids.at[spot], send_sem=ids_send,
            recv_sem=id_sem.at[spot], device_id=device(hub), device_id_type=MESH)

    def back_copy(spot):
        return pltpu.make_async_remote_copy(
            src_ref=maxima.at[spot], dst_ref=back, send_sem=back_send.at[spot],
            recv_sem=back_sem, device_id=device(spot), device_id_type=MESH)

    barrier = pltpu.get_barrier_semaphore()
    local_id_copy().start()
    local_copy().start()

    @pl.when(place != hub)
    def _():
        pl.semaphore_signal(barrier, inc=1, device_id=device(hub), device_id_type=MESH)
        local_id_copy().wait()
        local_copy().wait()
        block = normalize(raw[...])
        normed[slot(place), :] = block
        pl.semaphore_wait(barrier, 1)
        id_copy(place).start()
        row_copy(place).start()
        own_ids = ids[place]
        own = within(block, as_columns(own_ids), own_ids)
        id_copy(place).wait_send()
        row_copy(place).wait_send()
        back_copy(place).wait_recv()
        out_ref[...] = jnp.maximum(back[...], own)

    @pl.when(place == hub)
    def _():
        others = [spot for spot in range(span) if spot != hub]
        for spot in others:
            pl.semaphore_signal(barrier, inc=1, device_id=device(spot), device_id_type=MESH)
        local_id_copy().wait()
        local_copy().wait()
        order = sorted(range(span), key=lambda spot: (abs(spot - hub), -spot))
        row_ids = [ids[hub]]
        block = normalize(raw[...])
        normed[slot(hub), :] = block
        best = [within(block, as_columns(row_ids[0]), row_ids[0])]
        pl.semaphore_wait(barrier, span - 1)
        for spot in order[1:]:
            id_copy(spot).wait_recv()
            row_ids.append(ids[spot])
        column_ids = [as_columns(row) for row in row_ids]
        for step, spot in list(enumerate(order))[1:]:
            row_copy(spot).wait_recv()
            block = normed[slot(spot), :]
            last = step == span - 1
            if not last:
                scores = pair_scores(block, normed[pl.ds(0, step * rows), :])
            widest = None
            for other in (*range(1, step), 0):
                if last:
                    part = pair_scores(block, normed[slot(order[other]), :])
                else:
                    part = scores[:, other * rows:(other + 1) * rows]
                pairs = masked_pairs(part, column_ids[step], row_ids[other])
                best[other] = jnp.maximum(
                    best[other], jnp.max(pairs, axis=0, keepdims=True))
                widest = pairs if widest is None else jnp.maximum(widest, pairs)
                if last and other:
                    maxima[order[other]] = best[other]
                    back_copy(order[other]).start()
            best.append(jnp.max(jnp.transpose(widest), axis=0, keepdims=True))
        maxima[order[-1]] = best[-1]
        back_copy(order[-1]).start()
        out_ref[...] = best[0]
        for spot in others:
            back_copy(spot).wait_send()


def hub_device(span, embeddings, cluster_ids):
    _, rows, width = embeddings.shape
    return pl.pallas_call(
        functools.partial(hub_kernel, span),
        out_shape=pltpu.VMEM((1, rows), jnp.float32),
        in_specs=[pl.BlockSpec(memory_space=pl.ANY)] * 2,
        out_specs=pl.BlockSpec(memory_space=pltpu.VMEM),
        scratch_shapes=[
            pltpu.VMEM((rows, width), jnp.bfloat16),
            pltpu.VMEM((span, 1, rows), jnp.int32),
            pltpu.VMEM((span * rows, width), jnp.bfloat16),
            pltpu.VMEM((span, 1, rows), jnp.float32),
            pltpu.VMEM((1, rows), jnp.float32),
            pltpu.SemaphoreType.DMA,
            pltpu.SemaphoreType.DMA,
            pltpu.SemaphoreType.DMA,
            pltpu.SemaphoreType.DMA,
            pltpu.SemaphoreType.DMA((span,)),
            pltpu.SemaphoreType.DMA((span,)),
            pltpu.SemaphoreType.DMA((span,)),
            pltpu.SemaphoreType.DMA,
        ],
        compiler_params=pltpu.CompilerParams(
            collective_id=0, has_side_effects=True, vmem_limit_bytes=60 * 1024 * 1024),
    )(embeddings, cluster_ids)


def solution(mesh):
    span = mesh.shape["span"]
    body = functools.partial(hub_device, span) if 1 < span <= HUB_SPAN else gather_device
    return jax.shard_map(
        body,
        mesh=mesh,
        in_specs=(P(("groups", "batch"), "span", None), P(("groups", "batch"), "span")),
        out_specs=P(("groups", "batch"), "span"),
        check_vma=False,
    )
```

```python
import functools
import math

import jax
import jax.numpy as jnp
from jax import lax
from jax.experimental import pallas as pl
from jax.experimental.pallas import tpu as pltpu
from jax.sharding import PartitionSpec as P

MESH = pl.DeviceIdType.MESH
HUB_SPAN = 8


def normalize(embeddings):
    values = embeddings.astype(jnp.float32)
    inverse = lax.rsqrt(jnp.mean(values * values, axis=-1, keepdims=True) + 1e-06)
    return (values * inverse * (1.0 / math.sqrt(values.shape[-1]))).astype(jnp.bfloat16)


def pair_scores(left, right):
    return lax.dot_general(
        left, right, (((1,), (1,)), ((), ())), preferred_element_type=jnp.float32
    )


def gather_device(embeddings, cluster_ids):
    normed = normalize(embeddings[0])
    member_ids = cluster_ids[0]
    row_count = normed.shape[0]
    own_index = lax.axis_index("span")
    own_rows = own_index * row_count + jnp.arange(row_count, dtype=jnp.int32)
    piece_rows = lax.all_gather(normed, "span", axis=0, tiled=True)
    piece_ids = lax.all_gather(member_ids.astype(jnp.bfloat16), "span", axis=0, tiled=True)
    scores = pair_scores(normed, piece_rows)
    column_rows = jnp.arange(piece_rows.shape[0], dtype=jnp.int32)
    same_cluster = (member_ids[:, None] == piece_ids.astype(jnp.int32)[None, :]) & (
        own_rows[:, None] != column_rows[None, :]
    )
    nearest = jnp.max(jnp.where(same_cluster, scores, -1.0), axis=1)
    return jnp.maximum(nearest, -1.0)[None, :]


def masked_pairs(scores, column_ids, row_ids):
    return jnp.where(column_ids == row_ids, scores, -1.0)


def as_columns(row):
    return jnp.transpose(jnp.broadcast_to(row, (row.shape[1], row.shape[1])))


def within(block, column_ids, row_ids):
    rows = block.shape[0]
    apart = lax.broadcasted_iota(jnp.int32, (rows, rows), 0) != \
        lax.broadcasted_iota(jnp.int32, (rows, rows), 1)
    pairs = masked_pairs(pair_scores(block, block), column_ids, row_ids)
    return jnp.max(jnp.where(apart, pairs, -1.0), axis=0, keepdims=True)


def hub_kernel(span, emb_ref, ids_ref, out_ref, raw, ids, normed, maxima, back,
               local_sem, local_ids, send_sem, ids_send, row_sem, id_sem, back_send, back_sem):
    rows = emb_ref.shape[1]
    half = rows // 2
    me = lax.axis_index("span")
    flip = lax.rem(lax.axis_index("batch"), 2)
    place = jnp.where(flip == 1, me, span - 1 - me)
    hub = span // 2

    def slot(spot, piece=None):
        away = spot - hub
        if isinstance(spot, int):
            order = min(2 * away - 1 if away > 0 else -2 * away, span - 1)
            start = order * rows
            if piece is None:
                return pl.ds(start, rows)
            return pl.ds(start + piece * half, half)
        order = jnp.minimum(jnp.where(away > 0, 2 * away - 1, -2 * away), span - 1)
        if piece is None:
            return pl.ds(pl.multiple_of(order * rows, rows), rows)
        return pl.ds(pl.multiple_of(order * rows + piece * half, half), half)

    def device(spot):
        return {"span": jnp.where(flip == 1, spot, span - 1 - spot)}

    def local_copy():
        return pltpu.make_async_copy(emb_ref.at[0], raw, local_sem)

    def local_id_copy():
        return pltpu.make_async_copy(ids_ref, ids.at[place], local_ids)

    def row_copy(spot, piece):
        return pltpu.make_async_remote_copy(
            src_ref=normed.at[slot(spot, piece)], dst_ref=normed.at[slot(spot, piece)],
            send_sem=send_sem.at[piece],
            recv_sem=row_sem.at[spot, piece], device_id=device(hub), device_id_type=MESH)

    def id_copy(spot):
        return pltpu.make_async_remote_copy(
            src_ref=ids.at[spot], dst_ref=ids.at[spot], send_sem=ids_send,
            recv_sem=id_sem.at[spot], device_id=device(hub), device_id_type=MESH)

    def back_copy(spot):
        return pltpu.make_async_remote_copy(
            src_ref=maxima.at[spot], dst_ref=back, send_sem=back_send.at[spot],
            recv_sem=back_sem, device_id=device(spot), device_id_type=MESH)

    barrier = pltpu.get_barrier_semaphore()
    local_id_copy().start()
    local_copy().start()

    @pl.when(place != hub)
    def _():
        pl.semaphore_signal(barrier, inc=1, device_id=device(hub), device_id_type=MESH)
        local_id_copy().wait()
        local_copy().wait()
        pl.semaphore_wait(barrier, 1)
        id_copy(place).start()
        for piece in range(2):
            normed[slot(place, piece), :] = normalize(raw[pl.ds(piece * half, half), :])
            row_copy(place, piece).start()
        block = normed[slot(place), :]
        own_ids = ids[place]
        own = within(block, as_columns(own_ids), own_ids)
        id_copy(place).wait_send()
        for piece in range(2):
            row_copy(place, piece).wait_send()
        back_copy(place).wait_recv()
        out_ref[...] = jnp.maximum(back[...], own)

    @pl.when(place == hub)
    def _():
        others = [spot for spot in range(span) if spot != hub]
        for spot in others:
            pl.semaphore_signal(barrier, inc=1, device_id=device(spot), device_id_type=MESH)
        local_id_copy().wait()
        local_copy().wait()
        order = sorted(range(span), key=lambda spot: (abs(spot - hub), -spot))
        row_ids = [ids[hub]]
        block = normalize(raw[...])
        normed[slot(hub), :] = block
        best = [within(block, as_columns(row_ids[0]), row_ids[0])]
        pl.semaphore_wait(barrier, span - 1)
        for spot in order[1:]:
            id_copy(spot).wait_recv()
            row_ids.append(ids[spot])
        column_ids = [as_columns(row) for row in row_ids]
        for step, spot in list(enumerate(order))[1:]:
            for piece in range(2):
                row_copy(spot, piece).wait_recv()
            block = normed[slot(spot), :]
            last = step == span - 1
            if not last:
                scores = pair_scores(block, normed[pl.ds(0, step * rows), :])
            widest = None
            for other in (*range(1, step), 0):
                if last:
                    part = pair_scores(block, normed[slot(order[other]), :])
                else:
                    part = scores[:, other * rows:(other + 1) * rows]
                pairs = masked_pairs(part, column_ids[step], row_ids[other])
                best[other] = jnp.maximum(
                    best[other], jnp.max(pairs, axis=0, keepdims=True))
                widest = pairs if widest is None else jnp.maximum(widest, pairs)
                if last and other:
                    maxima[order[other]] = best[other]
                    back_copy(order[other]).start()
            best.append(jnp.max(jnp.transpose(widest), axis=0, keepdims=True))
        maxima[order[-1]] = best[-1]
        back_copy(order[-1]).start()
        out_ref[...] = best[0]
        for spot in others:
            back_copy(spot).wait_send()


def hub_device(span, embeddings, cluster_ids):
    _, rows, width = embeddings.shape
    return pl.pallas_call(
        functools.partial(hub_kernel, span),
        out_shape=pltpu.VMEM((1, rows), jnp.float32),
        in_specs=[pl.BlockSpec(memory_space=pl.ANY)] * 2,
        out_specs=pl.BlockSpec(memory_space=pltpu.VMEM),
        scratch_shapes=[
            pltpu.VMEM((rows, width), jnp.bfloat16),
            pltpu.VMEM((span, 1, rows), jnp.int32),
            pltpu.VMEM((span * rows, width), jnp.bfloat16),
            pltpu.VMEM((span, 1, rows), jnp.float32),
            pltpu.VMEM((1, rows), jnp.float32),
            pltpu.SemaphoreType.DMA,
            pltpu.SemaphoreType.DMA,
            pltpu.SemaphoreType.DMA((2,)),
            pltpu.SemaphoreType.DMA,
            pltpu.SemaphoreType.DMA((span, 2)),
            pltpu.SemaphoreType.DMA((span,)),
            pltpu.SemaphoreType.DMA((span,)),
            pltpu.SemaphoreType.DMA,
        ],
        compiler_params=pltpu.CompilerParams(
            collective_id=0, has_side_effects=True, vmem_limit_bytes=60 * 1024 * 1024),
    )(embeddings, cluster_ids)


def solution(mesh):
    span = mesh.shape["span"]
    body = functools.partial(hub_device, span) if 1 < span <= HUB_SPAN else gather_device
    return jax.shard_map(
        body,
        mesh=mesh,
        in_specs=(P(("groups", "batch"), "span", None), P(("groups", "batch"), "span")),
        out_specs=P(("groups", "batch"), "span"),
        check_vma=False,
    )
```
